32 devices in a mesh: leaf: 8 (over y, x, core), front: 4 (over z).
Axes of the slice: x: 2, y: 2, z: 4, core: 2. Of those that a mesh axis runs over, the one named last changes fastest.
Arguments:
- child_left_factors: bfloat16 [8, 6144, 128], P('leaf', 'front'), may hold values from -0.078125 to 0.078125
- child_v: bfloat16 [8, 6144, 128], P('leaf', 'front'), may hold values from -0.1875 to 0.1875
- ranks: int32 [8, 12], P('leaf', 'front'), may hold values from 8 to 128
- sketch: bfloat16 [6144, 128], P('front'), may hold values from -0.078125 to 0.078125
- dinv: bfloat16 [8, 12, 512, 512], P('leaf', 'front'), may hold values from -1 to 3, as said below
- rhs: bfloat16 [8, 64, 6144], P('leaf', None, 'front'), may hold values from -6 to 6
Outputs:
- solution: float32 [8, 64, 6144], P('leaf', None, 'front')
The draws below stay inside these ranges and needn't reach their ends.
Inputs may be any that keep to these rules, and one draw needn't show every extreme that they name: `ranks`: rank of each 512-row tile of a contribution block; columns of child_left_factors at or beyond it do not count. `dinv`: each [512, 512] block is the inverse of a diagonal tile of a factored front.
All inputs are finite; a program needn't handle non-finite values.
Results may differ from the reference program's by a relative error of at most 0.0045.
Values may be sent and summed in bfloat16 or wider, within the bound.
A program may use at most 64 MiB of HBM per device.

```python
import math
import jax
import jax.numpy as jnp
from jax import lax

TILE = 512
RANK = 128
RHS = 64
TILES = 12
FRONT = 6144
N_LEAF = 8


def draw_dinv(key, part):
    key = jax.random.fold_in(key, 11)
    first_key, second_key = jax.random.split(key)
    diagonal = jnp.exp(jax.random.uniform(first_key, (N_LEAF, TILES, TILE), jnp.float32, math.log(0.5), math.log(2.0)))
    spread = jnp.clip(jax.random.normal(second_key, (N_LEAF, TILES, TILE, TILE), jnp.float32), -4.0, 4.0)
    matrix = spread * (0.4 / math.sqrt(TILE)) + diagonal[..., None] * jnp.eye(TILE, dtype=jnp.float32)
    return matrix.astype(jnp.bfloat16)


def set_ends(drawn, key, least, top_value):
    longest = drawn.shape.index(max(drawn.shape))
    spots = []
    for shift in (0, 1):
        where = [jax.random.randint(jax.random.fold_in(key, axis), (), 0, length) for axis, length in enumerate(drawn.shape)]
        where[longest] = (where[longest] + shift) % drawn.shape[longest]
        spots.append(tuple(where))
    return drawn.at[spots[0]].set(least).at[spots[1]].set(top_value)


def block_scale(stream_key, dims, cuts, smallest, top_value):
    level, own = 1.0, jax.random.fold_in(stream_key, 6)
    for position, parts in cuts:
        steps = jnp.exp(jax.random.uniform(jax.random.fold_in(own, position), (parts,), jnp.float32, smallest / len(cuts), top_value / len(cuts)))
        level = level * jnp.repeat(steps, dims[position] // parts).reshape([-1 if axis == position else 1 for axis in range(len(dims))])
    return level


def centred(own_key, shape, width, bound, cuts=(), held_as=jnp.bfloat16):
    gain = block_scale(own_key, shape, cuts, -0.22, 0.18) if cuts else 1.0
    values = jax.random.normal(own_key, shape, jnp.float32) * width * gain
    return jnp.minimum(jnp.maximum(values, -bound), bound).astype(held_as)


def setup_inputs(seed: int = 0) -> dict:
    keys = jax.random.split(jax.random.key(seed), 7)
    return {
        "child_left_factors": centred(keys[0], (N_LEAF, FRONT, RANK), FRONT ** -0.5, 0.078125, ((0, 8), (1, 4))),
        "child_v": centred(keys[1], (N_LEAF, FRONT, RANK), (9 * RANK) ** -0.5, 0.1875, ((0, 8), (1, 4))),
        "ranks": set_ends(jax.random.randint(keys[2], (N_LEAF, TILES), RANK // 16, RANK + 1), jax.random.fold_in(keys[2], 1), RANK // 16, RANK).astype(jnp.int32),
        "sketch": centred(keys[3], (FRONT, RANK), FRONT ** -0.5, 0.078125, ((0, 4),)),
        "dinv": draw_dinv(jax.random.fold_in(keys[6], 71), 0),
        "rhs": centred(keys[5], (N_LEAF, RHS, FRONT), 1.0, 6.0, ((0, 8), (2, 4))),
    }


def masked_rows(child_left_factors, ranks):
    tile = child_left_factors.shape[1] // ranks.shape[1]
    rank_of_rows = jnp.repeat(ranks, tile, axis=1)
    keep = lax.broadcasted_iota(jnp.int32, child_left_factors.shape, 2) < rank_of_rows[:, :, None]
    return jnp.where(keep, child_left_factors, jnp.zeros_like(child_left_factors))

def block_product(form, left, right):
    return jnp.einsum(form, left.astype(jnp.float32), right.astype(jnp.float32), precision=lax.Precision.HIGHEST)

def rounded(value):
    return lax.optimization_barrier(value.astype(jnp.bfloat16))

def right_solve(factor, matrix):
    return jax.vmap(lambda factor_one, block_one: jax.scipy.linalg.solve_triangular(factor_one, block_one.T, lower=True).T)(factor, matrix)

def merge_pairs(first_u, first_v, second_u, second_v, sketch):
    proj_first = rounded(block_product('kmr,ms->krs', first_v, sketch))
    proj_second = rounded(block_product('kmr,ms->krs', second_v, sketch))
    sample = block_product('kmr,krs->kms', first_u, proj_first) + block_product('kmr,krs->kms', second_u, proj_second)
    gram = block_product('kms,kmt->kst', sample, sample)
    factor = jnp.linalg.cholesky(gram)
    basis = right_solve(factor, sample)
    weight_first = rounded(block_product('kmr,kms->krs', first_u, basis))
    second_weight = rounded(block_product('kmr,kms->krs', second_u, basis))
    new_v = block_product('kmr,krs->kms', first_v, weight_first) + block_product('kmr,krs->kms', second_v, second_weight)
    return (basis.astype(jnp.bfloat16), new_v.astype(jnp.bfloat16))

def reference(child_left_factors, child_v, ranks, sketch, dinv, rhs):
    own_u = masked_rows(child_left_factors, ranks)
    pair_u, pair_v = merge_pairs(own_u[0::2], child_v[0::2], own_u[1::2], child_v[1::2], sketch)
    group_u, group_v = merge_pairs(pair_u[0::2], pair_v[0::2], pair_u[1::2], pair_v[1::2], sketch)
    group_u = jnp.repeat(group_u, 4, axis=0)
    group_v = jnp.repeat(group_v, 4, axis=0)

    def prepare(inputs):
        tile_inv, left_f, right_f, sides = inputs
        coupled_blocks = block_product('tij,tjr->tir', tile_inv, left_f.reshape(TILES, TILE, RANK)).reshape(FRONT, RANK)
        coupled_blocks = rounded(coupled_blocks)
        solved_rows = block_product('htj,tij->hti', sides.reshape(RHS, TILES, TILE), tile_inv).reshape(RHS, FRONT)
        solved_b = rounded(solved_rows)
        matrix = block_product('mr,ms->rs', right_f, coupled_blocks)
        vector = block_product('hm,mr->hr', solved_b, right_f)
        return (coupled_blocks, solved_rows, matrix, vector)
    coupled_blocks, solved_rows, matrix, vector = lax.map(prepare, (dinv, group_u, group_v, rhs))

    def advance(state, inputs):
        matrix_one, vector_one = inputs
        fresh = vector_one - jnp.dot(state, matrix_one.T, precision=lax.Precision.HIGHEST)
        return (fresh, state)
    start = jnp.zeros((RHS, RANK), jnp.float32)
    _, previous = lax.scan(advance, start, (matrix, vector))
    return solved_rows - block_product('cok,cnk->con', previous, coupled_blocks)
```

```python
import functools

import jax
import jax.numpy as jnp
from jax import lax
from jax.experimental import pallas as pl
from jax.experimental.pallas import tpu as pltpu
from jax.sharding import PartitionSpec as P

MESH = pl.DeviceIdType.MESH
F32 = jnp.float32
BF16 = jnp.bfloat16
PANEL = 8


def dot(a, b):
    return jnp.dot(a, b, preferred_element_type=F32)


def dot_nt(a, b):
    return lax.dot_general(a, b, (((1,), (1,)), ((), ())), preferred_element_type=F32)


def dot_tn(a, b):
    return lax.dot_general(a, b, (((0,), (0,)), ((), ())), preferred_element_type=F32)


def full(a, b, ca=1, cb=0):
    return lax.dot_general(
        a,
        b,
        (((ca,), (cb,)), ((), ())),
        precision=lax.Precision.HIGHEST,
        preferred_element_type=F32,
    )


def halves(x):
    high = x.astype(BF16)
    return high, (x - high.astype(F32)).astype(BF16)


def flip(index, bit):
    return index + bit - 2 * bit * lax.rem(index // bit, 2)


def inverse_factors(grams, work, inverse):
    size = grams[0].shape[0]
    eye = (
        lax.broadcasted_iota(jnp.int32, (size, size), 0)
        == lax.broadcasted_iota(jnp.int32, (size, size), 1)
    ).astype(F32)
    for q, gram in enumerate(grams):
        work[q, :, :size] = gram
        work[q, :, size:] = eye
    lane = lax.broadcasted_iota(jnp.int32, (PANEL, size), 1)
    row = lax.broadcasted_iota(jnp.int32, (PANEL, size), 0)

    def step(b, carry):
        base = pl.multiple_of(b * PANEL, PANEL)
        for q in range(len(grams)):
            left = work[q, pl.ds(base, PANEL), :size]
            right = work[q, pl.ds(base, PANEL), size:]
            columns = [
                jnp.broadcast_to(
                    jnp.sum(jnp.where(lane == base + j, left, 0.0), axis=1, keepdims=True),
                    (PANEL, size),
                )
                for j in range(PANEL)
            ]
            pivots = jnp.zeros((PANEL, size), F32)
            for j in range(PANEL):
                pivots = jnp.where(row == j, columns[j], pivots)
                times = jnp.where(row > j, columns[j] * (1.0 / columns[j][j : j + 1, :]), 0.0)
                left = left - times * left[j : j + 1, :]
                right = right - times * right[j : j + 1, :]
                for k in range(j + 1, PANEL):
                    columns[k] = columns[k] - times * columns[k][j : j + 1, :]
            scale = lax.rsqrt(pivots)
            scale = scale * (1.5 - 0.5 * pivots * scale * scale)
            left = left * scale
            right = right * scale
            inverse[q, pl.ds(base, PANEL), :] = right
            below = jnp.where(lane >= base + PANEL, left, 0.0)
            work[q] -= full(below, jnp.concatenate([left, right], axis=1), 0, 0)
        return carry

    lax.fori_loop(0, size // PANEL, step, 0)


def kernel(
    leaves, fronts, rank_ref, u_ref, v_ref, sketch_ref, dinv_ref, rhs_ref, out_ref,
    uall, vall, strip, landed, gath, work, inverse, wide, part, landed2, whole, hyper, sol,
    a_send, a_recv, rs_send, rs_recv, ag_send, ag_recv, d_send, d_recv,
    rs2_send, rs2_recv, ag2_send, ag2_recv, h_send, h_recv,
):
    leaf = lax.axis_index("leaf")
    front = lax.axis_index("front")
    tiles, tile = dinv_ref.shape[1], dinv_ref.shape[2]
    rank = u_ref.shape[2]
    sides = rhs_ref.shape[1]
    levels = leaves.bit_length() - 1
    mine = lax.rem(leaf, 4)
    sibling, cousin = flip(leaf, 1), flip(leaf, 2)
    theirs, across = flip(mine, 1), flip(mine, 2)
    opposite = flip(theirs, 2)
    shard = strip.shape[0] // fronts
    shard2 = part.shape[0] // fronts

    barrier = pltpu.get_barrier_semaphore()
    for level in range(levels):
        pl.semaphore_signal(barrier, inc=1, device_id=(flip(leaf, 1 << level), front), device_id_type=MESH)
    for d in range(1, fronts):
        pl.semaphore_signal(barrier, inc=1, device_id=(leaf, lax.rem(front + d, fronts)), device_id_type=MESH)

    def rows(t):
        return pl.ds(t * tile, tile)

    column = lax.broadcasted_iota(jnp.int32, (tile, rank), 1)
    for t in range(tiles):
        keep = column < rank_ref[0, t]
        uall[mine, rows(t), :] = jnp.where(keep, u_ref[0, rows(t), :].astype(F32), 0.0).astype(BF16)
        vall[mine, rows(t), :] = v_ref[0, rows(t), :]
    pl.semaphore_wait(barrier, levels + fronts - 1)

    def remote(src, dst, send, recv, target):
        return pltpu.make_async_remote_copy(
            src_ref=src, dst_ref=dst, send_sem=send, recv_sem=recv, device_id=target, device_id_type=MESH
        )

    def factor_copy(kind, path, t):
        held = (uall, vall)[kind]
        block = held.at[across if path == 2 else mine, rows(t), :]
        target = (cousin if path == 1 else sibling, front)
        return remote(block, block, a_send.at[kind, path, t], a_recv.at[kind, path, t], target)

    for kind in range(2):
        for path in (1, 0):
            for t in range(tiles):
                factor_copy(kind, path, t).start()

    def scatter_copy(f, buffer, landing, size, send, recv):
        return remote(buffer.at[pl.ds(f * size, size), :], landing.at[front], send.at[f], recv.at[front], (leaf, f))

    def landing_wait(s, buffer, landing, size, send, recv):
        remote(buffer.at[pl.ds(0, size), :], landing.at[s], send.at[s], recv.at[s], (leaf, s)).wait_recv()

    first = (strip, landed, shard, rs_send, rs_recv)
    second = (part, landed2, shard2, rs2_send, rs2_recv)

    def scatter(lower, upper, what):
        for f in range(lower, upper):
            @pl.when(front != f)
            def _(f=f):
                scatter_copy(f, *what).start()

    own_t = uall[mine].T
    strip[pl.ds(0, rank), :] = dot_tn(vall[mine], sketch_ref[...])
    scatter(0, fronts // 4, first)
    strip[pl.ds(rank, rank), :] = dot(own_t, uall[mine])
    scatter(fronts // 4, fronts // 2, first)

    for t in range(tiles):
        sol[:, rows(t)] = dot_nt(rhs_ref[0, :, rows(t)], dinv_ref[0, t])

    for t in range(tiles):
        factor_copy(0, 1, t).wait_recv()
        factor_copy(0, 2, t).start()
    for t in range(tiles):
        factor_copy(0, 0, t).wait_recv()
    for t in range(tiles):
        factor_copy(0, 2, t).wait_recv()
    for j in (1, 2):
        strip[pl.ds((j + 1) * rank, rank), :] = dot(own_t, uall[lax.rem(mine + j, 4)])
        scatter((j + 1) * fronts // 4, (j + 2) * fronts // 4, first)

    def reduced(buffer, landing, size, send, recv):
        total = buffer[pl.ds(pl.multiple_of(front * size, 8), size), :]
        for s in range(fronts):
            @pl.when(front != s)
            def _(s=s):
                landing_wait(s, buffer, landing, size, send, recv)

            total = total + jnp.where(front != s, landing[s], 0.0)
        return total

    for s in range(fronts):
        @pl.when(front == s)
        def _(s=s):
            landed[s] = jnp.zeros(landed.shape[1:], F32)
            landed2[s] = jnp.zeros(landed2.shape[1:], F32)

    def piece(i, s):
        return gath.at[i, pl.ds(s * shard, shard), :]

    def gather_copy(d):
        return remote(
            piece(mine, front), piece(mine, front), ag_send.at[d], ag_recv.at[d], (leaf, lax.rem(front + d, fronts))
        )

    def spread_copy(path, d):
        block = piece(across if path == 2 else mine, lax.rem(front - d + fronts, fronts))
        target = (cousin if path == 1 else sibling, front)
        return remote(block, block, d_send.at[path, d], d_recv.at[path, d], target)

    gath[mine, pl.ds(pl.multiple_of(front * shard, 8), shard), :] = reduced(*first)
    for d in range(1, fronts):
        gather_copy(d).start()
    for d in range(fronts):
        if d:
            gather_copy(d).wait_recv()
        spread_copy(1, d).start()
        spread_copy(0, d).start()
    for t in range(tiles):
        factor_copy(1, 1, t).wait_recv()
        factor_copy(1, 2, t).start()
    for d in range(fronts):
        spread_copy(1, d).wait_recv()
        spread_copy(2, d).start()
    for d in range(fronts):
        spread_copy(0, d).wait_recv()
    for d in range(fronts):
        spread_copy(2, d).wait_recv()

    def block(i, j):
        return gath[i, pl.ds(j * rank, rank), :]

    def square(a, b, c, d):
        wide[pl.ds(0, rank), pl.ds(0, rank)] = a
        wide[pl.ds(0, rank), pl.ds(rank, rank)] = b
        wide[pl.ds(rank, rank), pl.ds(0, rank)] = c
        wide[pl.ds(rank, rank), pl.ds(rank, rank)] = d
        return wide[...]

    raw, small, cross, grams = [], [], [], []
    for p in range(2):
        a, b = 2 * p, 2 * p + 1
        between = block(a, 2)
        pair = square(block(a, 1), between, between.T, block(b, 1))
        raw.append(jnp.concatenate([block(a, 0), block(b, 0)], axis=0))
        small.append(raw[p].astype(BF16).astype(F32))
        cross.append(full(pair, small[p]))
        grams.append(full(small[p], cross[p], 0, 0))
    inverse_factors(grams, work, inverse)
    turn = [full(small[p], inverse[p], 1, 1) for p in range(2)]
    weight = [full(cross[p], inverse[p], 1, 1).astype(BF16).astype(F32) for p in range(2)]
    small2 = [full(weight[p], raw[p], 0, 0).astype(BF16).astype(F32) for p in range(2)]
    pair = square(block(0, 3), block(3, 2).T, block(1, 2), block(1, 3))
    middle = full(turn[0], full(pair, turn[1]), 0, 0)
    cross2 = [small2[0] + full(middle, small2[1]), full(middle, small2[0], 0, 0) + small2[1]]
    gram2 = full(small2[0], cross2[0], 0, 0) + full(small2[1], cross2[1], 0, 0)
    inverse_factors([gram2], work, inverse)
    turn2 = [halves(full(turn[p], full(small2[p], inverse[0], 1, 1))) for p in range(2)]
    weight2 = [
        halves(full(weight[p], full(cross2[p], inverse[0], 1, 1).astype(BF16).astype(F32))) for p in range(2)
    ]

    def combined(held, factors):
        total = None
        for i in range(4):
            half = slice((i % 2) * rank, (i % 2 + 1) * rank)
            for part_of in factors[i // 2]:
                term = dot(held[i], part_of[half])
                total = term if total is None else total + term
        return total.astype(BF16)

    left_f = combined(uall, turn2)
    coupled = [dot(dinv_ref[0, t], left_f[t * tile : (t + 1) * tile]).astype(BF16) for t in range(tiles)]
    for path in (0, 2):
        for t in range(tiles):
            factor_copy(1, path, t).wait_recv()
    right_f = combined(vall, weight2)
    used = rank + sides
    if used < part.shape[0]:
        part[pl.ds(used, part.shape[0] - used), :] = jnp.zeros((part.shape[0] - used, rank), F32)
    part[pl.ds(0, rank), :] = -dot_tn(jnp.concatenate(coupled, axis=0), right_f)
    part[pl.ds(rank, sides), :] = dot(sol[...].astype(BF16), right_f)

    scatter(0, fronts, second)

    def piece2(s):
        return whole.at[pl.ds(s * shard2, shard2), :]

    def gather2_copy(d):
        return remote(
            piece2(front), piece2(front), ag2_send.at[d], ag2_recv.at[d], (leaf, lax.rem(front + d, fronts))
        )

    whole[pl.ds(pl.multiple_of(front * shard2, 8), shard2), :] = reduced(*second)
    for d in range(1, fronts):
        gather2_copy(d).start()
    for d in range(1, fronts):
        gather2_copy(d).wait_recv()

    hyper[0, 0] = whole[pl.ds(0, used), :]
    low = lax.broadcasted_iota(jnp.int32, (used, rank), 0)
    along = lax.broadcasted_iota(jnp.int32, (used, rank), 1)
    prefix = jnp.where(low == along, 1.0, 0.0)

    def then(first_map, second_map):
        return full(first_map, second_map[:rank]) + jnp.where(low >= rank, second_map, 0.0)

    def hyper_copy(k):
        send = pl.ds(0, used) if k < levels - 1 else pl.ds(rank, sides)
        return remote(
            hyper.at[k, 0, send, :], hyper.at[k, 1, send, :], h_send.at[k], h_recv.at[k], (flip(leaf, 1 << k), front)
        )

    previous = None
    for k in range(levels):
        hyper_copy(k).start()
        hyper_copy(k).wait_recv()
        upper = lax.rem(leaf // (1 << k), 2) == 1
        if k < levels - 1:
            here, there = hyper[k, 0], hyper[k, 1]
            hyper[k + 1, 0] = then(jnp.where(upper, there, here), jnp.where(upper, here, there))
            prefix = jnp.where(upper, then(there, prefix), prefix)
        else:
            there = hyper[k, 1, pl.ds(rank, sides), :]
            previous = prefix[rank:] + jnp.where(upper, full(there, prefix[:rank]), 0.0)

    for t in range(tiles):
        total = sol[:, rows(t)]
        for part_of in halves(previous):
            total = total - dot_nt(part_of, coupled[t])
        out_ref[0, :, rows(t)] = total

    for kind in range(2):
        for path in range(3):
            for t in range(tiles):
                factor_copy(kind, path, t).wait_send()
    for f in range(fronts):
        @pl.when(front != f)
        def _(f=f):
            scatter_copy(f, *first).wait_send()
            scatter_copy(f, *second).wait_send()
    for d in range(1, fronts):
        gather_copy(d).wait_send()
        gather2_copy(d).wait_send()
    for path in range(3):
        for d in range(fronts):
            spread_copy(path, d).wait_send()
    for k in range(levels):
        hyper_copy(k).wait_send()


def solution(mesh):
    leaves, fronts = mesh.shape["leaf"], mesh.shape["front"]
    levels = leaves.bit_length() - 1

    def on_device(child_left_factors, child_v, ranks, sketch, dinv, rhs):
        _, length, rank = child_left_factors.shape
        tiles = dinv.shape[1]
        sides = rhs.shape[1]
        used = rank + sides
        shard = 4 * rank // fronts
        shard2 = -(-used // (8 * fronts)) * 8
        vmem = pl.BlockSpec(memory_space=pltpu.VMEM)
        dma = pltpu.SemaphoreType.DMA
        return pl.pallas_call(
            functools.partial(kernel, leaves, fronts),
            out_shape=jax.ShapeDtypeStruct((1, sides, length), F32),
            in_specs=[pl.BlockSpec(memory_space=pltpu.SMEM)] + [vmem] * 5,
            out_specs=vmem,
            scratch_shapes=[
                pltpu.VMEM((4, length, rank), BF16),
                pltpu.VMEM((4, length, rank), BF16),
                pltpu.VMEM((4 * rank, rank), F32),
                pltpu.VMEM((fronts, shard, rank), F32),
                pltpu.VMEM((4, 4 * rank, rank), F32),
                pltpu.VMEM((2, rank, 2 * rank), F32),
                pltpu.VMEM((2, rank, rank), F32),
                pltpu.VMEM((2 * rank, 2 * rank), F32),
                pltpu.VMEM((shard2 * fronts, rank), F32),
                pltpu.VMEM((fronts, shard2, rank), F32),
                pltpu.VMEM((shard2 * fronts, rank), F32),
                pltpu.VMEM((levels, 2, used, rank), F32),
                pltpu.VMEM((sides, length), F32),
                dma((2, 3, tiles)),
                dma((2, 3, tiles)),
                dma((fronts,)),
                dma((fronts,)),
                dma((fronts,)),
                dma((fronts,)),
                dma((3, fronts)),
                dma((3, fronts)),
                dma((fronts,)),
                dma((fronts,)),
                dma((fronts,)),
                dma((fronts,)),
                dma((levels,)),
                dma((levels,)),
            ],
            compiler_params=pltpu.CompilerParams(
                collective_id=0, has_side_effects=True, vmem_limit_bytes=40 * 1024 * 1024
            ),
        )(ranks, child_left_factors, child_v, sketch, dinv, rhs)

    placed = (
        P("leaf", "front", None),
        P("leaf", "front", None),
        P("leaf", "front"),
        P("front", None),
        P("leaf", "front", None, None),
        P("leaf", None, "front"),
    )
    return jax.shard_map(
        on_device, mesh=mesh, in_specs=placed, out_specs=P("leaf", None, "front"), check_vma=False
    )
```

```python
import functools

import jax
import jax.numpy as jnp
from jax import lax
from jax.experimental import pallas as pl
from jax.experimental.pallas import tpu as pltpu
from jax.sharding import PartitionSpec as P

MESH = pl.DeviceIdType.MESH
F32 = jnp.float32
BF16 = jnp.bfloat16
PANEL = 16


def dot(a, b):
    return jnp.dot(a, b, preferred_element_type=F32)


def dot_nt(a, b):
    return lax.dot_general(a, b, (((1,), (1,)), ((), ())), preferred_element_type=F32)


def dot_tn(a, b):
    return lax.dot_general(a, b, (((0,), (0,)), ((), ())), preferred_element_type=F32)


def thirds(x):
    high = x.astype(BF16)
    rest = x - high.astype(F32)
    middle = rest.astype(BF16)
    return high, middle, (rest - middle.astype(F32)).astype(BF16)


def full(a, b, ca=1, cb=0):
    if a.dtype == BF16:
        pa, pb = [a] * 3, thirds(b)
    elif b.dtype == BF16:
        pa, pb = thirds(a), [b] * 3
    else:
        (a1, a2, a3), (b1, b2, b3) = thirds(a), thirds(b)
        pa, pb = (a1, a2, a1, a3, a2, a1), (b1, b1, b2, b1, b2, b3)
    return lax.dot_general(
        jnp.concatenate(pa, axis=ca),
        jnp.concatenate(pb, axis=cb),
        (((ca,), (cb,)), ((), ())),
        preferred_element_type=F32,
    )


def halves(x):
    high = x.astype(BF16)
    return high, (x - high.astype(F32)).astype(BF16)


def flip(index, bit):
    return index + bit - 2 * bit * lax.rem(index // bit, 2)


def inverse_factors(grams, work, inverse):
    size = grams[0].shape[0]
    eye = (
        lax.broadcasted_iota(jnp.int32, (size, size), 0)
        == lax.broadcasted_iota(jnp.int32, (size, size), 1)
    ).astype(F32)
    for q, gram in enumerate(grams):
        work[q, :, :size] = gram
        work[q, :, size:] = eye
    lane = lax.broadcasted_iota(jnp.int32, (PANEL, size), 1)
    row = lax.broadcasted_iota(jnp.int32, (PANEL, size), 0)

    def step(b, carry):
        base = pl.multiple_of(b * PANEL, PANEL)
        for q in range(len(grams)):
            left = work[q, pl.ds(base, PANEL), :size]
            right = work[q, pl.ds(base, PANEL), size:]
            columns = [
                jnp.broadcast_to(
                    jnp.sum(jnp.where(lane == base + j, left, 0.0), axis=1, keepdims=True),
                    (PANEL, size),
                )
                for j in range(PANEL)
            ]
            pivots = jnp.zeros((PANEL, size), F32)
            for j in range(PANEL):
                pivots = jnp.where(row == j, columns[j], pivots)
                times = jnp.where(row > j, columns[j] * (1.0 / columns[j][j : j + 1, :]), 0.0)
                left = left - times * left[j : j + 1, :]
                right = right - times * right[j : j + 1, :]
                for k in range(j + 1, PANEL):
                    columns[k] = columns[k] - times * columns[k][j : j + 1, :]
            scale = lax.rsqrt(pivots)
            scale = scale * (1.5 - 0.5 * pivots * scale * scale)
            left = left * scale
            right = right * scale
            inverse[q, pl.ds(base, PANEL), :] = right
            below = jnp.where(lane >= base + PANEL, left, 0.0)
            work[q] -= full(below, jnp.concatenate([left, right], axis=1), 0, 0)
        return carry

    lax.fori_loop(0, size // PANEL, step, 0, unroll=True)


def kernel(
    leaves, fronts, rank_ref, u_ref, v_ref, sketch_ref, dinv_ref, rhs_ref, out_ref,
    uall, vall, strip, landed, gath, work, inverse, wide, part, landed2, whole, hyper, sol,
    a_send, a_recv, rs_send, rs_recv, ag_send, ag_recv, d_send, d_recv,
    rs2_send, rs2_recv, ag2_send, ag2_recv, h_send, h_recv,
):
    leaf = lax.axis_index("leaf")
    front = lax.axis_index("front")
    tiles, tile = dinv_ref.shape[1], dinv_ref.shape[2]
    rank = u_ref.shape[2]
    sides = rhs_ref.shape[1]
    levels = leaves.bit_length() - 1
    mine = lax.rem(leaf, 4)
    sibling, cousin = flip(leaf, 1), flip(leaf, 2)
    theirs, across = flip(mine, 1), flip(mine, 2)
    opposite = flip(theirs, 2)
    shard = strip.shape[0] // fronts
    shard2 = part.shape[0] // fronts

    barrier = pltpu.get_barrier_semaphore()
    for level in range(levels):
        pl.semaphore_signal(barrier, inc=1, device_id=(flip(leaf, 1 << level), front), device_id_type=MESH)
    for d in range(1, fronts):
        pl.semaphore_signal(barrier, inc=1, device_id=(leaf, lax.rem(front + d, fronts)), device_id_type=MESH)

    def rows(t):
        return pl.ds(t * tile, tile)

    column = lax.broadcasted_iota(jnp.int32, (tile, rank), 1)
    for t in range(tiles):
        keep = column < rank_ref[0, t]
        uall[mine, rows(t), :] = jnp.where(keep, u_ref[0, rows(t), :].astype(F32), 0.0).astype(BF16)
        vall[mine, rows(t), :] = v_ref[0, rows(t), :]
    pl.semaphore_wait(barrier, levels + fronts - 1)

    def remote(src, dst, send, recv, target):
        return pltpu.make_async_remote_copy(
            src_ref=src, dst_ref=dst, send_sem=send, recv_sem=recv, device_id=target, device_id_type=MESH
        )

    def factor_copy(kind, path, t):
        held = (uall, vall)[kind]
        block = held.at[across if path == 2 else mine, rows(t), :]
        target = (cousin if path == 1 else sibling, front)
        return remote(block, block, a_send.at[kind, path, t], a_recv.at[kind, path, t], target)

    for kind in range(2):
        for path in (1, 0):
            for t in range(tiles):
                factor_copy(kind, path, t).start()

    def scatter_copy(f, buffer, landing, size, send, recv):
        return remote(buffer.at[pl.ds(f * size, size), :], landing.at[front], send.at[f], recv.at[front], (leaf, f))

    def landing_wait(s, buffer, landing, size, send, recv):
        remote(buffer.at[pl.ds(0, size), :], landing.at[s], send.at[s], recv.at[s], (leaf, s)).wait_recv()

    first = (strip, landed, shard, rs_send, rs_recv)
    second = (part, landed2, shard2, rs2_send, rs2_recv)

    def scatter(lower, upper, what):
        for f in range(lower, upper):
            @pl.when(front != f)
            def _(f=f):
                scatter_copy(f, *what).start()

    own_t = uall[mine].T
    strip[pl.ds(0, rank), :] = dot_tn(vall[mine], sketch_ref[...])
    scatter(0, fronts // 4, first)
    strip[pl.ds(rank, rank), :] = dot(own_t, uall[mine])
    scatter(fronts // 4, fronts // 2, first)

    for t in range(tiles):
        sol[:, rows(t)] = dot_nt(rhs_ref[0, :, rows(t)], dinv_ref[0, t])

    for t in range(tiles):
        factor_copy(0, 1, t).wait_recv()
        factor_copy(0, 2, t).start()
    for t in range(tiles):
        factor_copy(0, 0, t).wait_recv()
    for t in range(tiles):
        factor_copy(0, 2, t).wait_recv()
    for j in (1, 2):
        strip[pl.ds((j + 1) * rank, rank), :] = dot(own_t, uall[lax.rem(mine + j, 4)])
        scatter((j + 1) * fronts // 4, (j + 2) * fronts // 4, first)

    def reduced(buffer, landing, size, send, recv):
        total = buffer[pl.ds(pl.multiple_of(front * size, 8), size), :]
        for s in range(fronts):
            @pl.when(front != s)
            def _(s=s):
                landing_wait(s, buffer, landing, size, send, recv)

            total = total + jnp.where(front != s, landing[s], 0.0)
        return total

    for s in range(fronts):
        @pl.when(front == s)
        def _(s=s):
            landed[s] = jnp.zeros(landed.shape[1:], F32)
            landed2[s] = jnp.zeros(landed2.shape[1:], F32)

    def piece(i, s):
        return gath.at[i, pl.ds(s * shard, shard), :]

    def gather_copy(d):
        return remote(
            piece(mine, front), piece(mine, front), ag_send.at[d], ag_recv.at[d], (leaf, lax.rem(front + d, fronts))
        )

    def spread_copy(path, d):
        block = piece(across if path == 2 else mine, lax.rem(front - d + fronts, fronts))
        target = (cousin if path == 1 else sibling, front)
        return remote(block, block, d_send.at[path, d], d_recv.at[path, d], target)

    gath[mine, pl.ds(pl.multiple_of(front * shard, 8), shard), :] = reduced(*first)
    for d in range(1, fronts):
        gather_copy(d).start()
    for d in range(fronts):
        if d:
            gather_copy(d).wait_recv()
        spread_copy(1, d).start()
        spread_copy(0, d).start()
    for t in range(tiles):
        factor_copy(1, 1, t).wait_recv()
        factor_copy(1, 2, t).start()
    for d in range(fronts):
        spread_copy(1, d).wait_recv()
        spread_copy(2, d).start()
    for d in range(fronts):
        spread_copy(0, d).wait_recv()
    for d in range(fronts):
        spread_copy(2, d).wait_recv()

    def block(i, j):
        return gath[i, pl.ds(j * rank, rank), :]

    def square(a, b, c, d):
        wide[pl.ds(0, rank), pl.ds(0, rank)] = a
        wide[pl.ds(0, rank), pl.ds(rank, rank)] = b
        wide[pl.ds(rank, rank), pl.ds(0, rank)] = c
        wide[pl.ds(rank, rank), pl.ds(rank, rank)] = d
        return wide[...]

    raw, small, cross, grams = [], [], [], []
    for p in range(2):
        a, b = 2 * p, 2 * p + 1
        between = block(a, 2)
        pair = square(block(a, 1), between, between.T, block(b, 1))
        raw.append(jnp.concatenate([block(a, 0), block(b, 0)], axis=0))
        small.append(raw[p].astype(BF16))
        cross.append(full(pair, small[p]))
        grams.append(full(small[p], cross[p], 0, 0))
    inverse_factors(grams, work, inverse)
    turn = [full(small[p], inverse[p], 1, 1) for p in range(2)]
    weight = [full(cross[p], inverse[p], 1, 1).astype(BF16) for p in range(2)]
    small2 = [full(weight[p], raw[p], 0, 0).astype(BF16) for p in range(2)]
    pair = square(block(0, 3), block(3, 2).T, block(1, 2), block(1, 3))
    middle = full(turn[0], full(pair, turn[1]), 0, 0)
    cross2 = [small2[0].astype(F32) + full(middle, small2[1]), full(middle, small2[0], 0, 0) + small2[1].astype(F32)]
    gram2 = full(small2[0], cross2[0], 0, 0) + full(small2[1], cross2[1], 0, 0)
    inverse_factors([gram2], work, inverse)
    turn2 = [halves(full(turn[p], full(small2[p], inverse[0], 1, 1))) for p in range(2)]
    weight2 = [
        halves(dot(weight[p], full(cross2[p], inverse[0], 1, 1).astype(BF16))) for p in range(2)
    ]

    def combined(held, factors):
        total = None
        for i in range(4):
            half = slice((i % 2) * rank, (i % 2 + 1) * rank)
            for part_of in factors[i // 2]:
                term = dot(held[i], part_of[half])
                total = term if total is None else total + term
        return total.astype(BF16)

    left_f = combined(uall, turn2)
    coupled = [dot(dinv_ref[0, t], left_f[t * tile : (t + 1) * tile]).astype(BF16) for t in range(tiles)]
    for path in (0, 2):
        for t in range(tiles):
            factor_copy(1, path, t).wait_recv()
    right_f = combined(vall, weight2)
    used = rank + sides
    if used < part.shape[0]:
        part[pl.ds(used, part.shape[0] - used), :] = jnp.zeros((part.shape[0] - used, rank), F32)
    part[pl.ds(0, rank), :] = -dot_tn(jnp.concatenate(coupled, axis=0), right_f)
    part[pl.ds(rank, sides), :] = dot(sol[...].astype(BF16), right_f)

    scatter(0, fronts, second)

    def piece2(s):
        return whole.at[pl.ds(s * shard2, shard2), :]

    def gather2_copy(d):
        return remote(
            piece2(front), piece2(front), ag2_send.at[d], ag2_recv.at[d], (leaf, lax.rem(front + d, fronts))
        )

    whole[pl.ds(pl.multiple_of(front * shard2, 8), shard2), :] = reduced(*second)
    for d in range(1, fronts):
        gather2_copy(d).start()
    for d in range(1, fronts):
        gather2_copy(d).wait_recv()

    hyper[0, 0] = whole[pl.ds(0, used), :]
    low = lax.broadcasted_iota(jnp.int32, (used, rank), 0)
    along = lax.broadcasted_iota(jnp.int32, (used, rank), 1)
    prefix = jnp.where(low == along, 1.0, 0.0)

    def then(first_map, second_map):
        return full(first_map, second_map[:rank]) + jnp.where(low >= rank, second_map, 0.0)

    def hyper_copy(k):
        send = pl.ds(0, used) if k < levels - 1 else pl.ds(rank, sides)
        return remote(
            hyper.at[k, 0, send, :], hyper.at[k, 1, send, :], h_send.at[k], h_recv.at[k], (flip(leaf, 1 << k), front)
        )

    previous = None
    for k in range(levels):
        hyper_copy(k).start()
        hyper_copy(k).wait_recv()
        upper = lax.rem(leaf // (1 << k), 2) == 1
        if k < levels - 1:
            here, there = hyper[k, 0], hyper[k, 1]
            hyper[k + 1, 0] = then(jnp.where(upper, there, here), jnp.where(upper, here, there))
            prefix = jnp.where(upper, then(there, prefix), prefix)
        else:
            there = hyper[k, 1, pl.ds(rank, sides), :]
            previous = prefix[rank:] + jnp.where(upper, full(there, prefix[:rank]), 0.0)

    for t in range(tiles):
        total = sol[:, rows(t)]
        for part_of in halves(previous):
            total = total - dot_nt(part_of, coupled[t])
        out_ref[0, :, rows(t)] = total

    for kind in range(2):
        for path in range(3):
            for t in range(tiles):
                factor_copy(kind, path, t).wait_send()
    for f in range(fronts):
        @pl.when(front != f)
        def _(f=f):
            scatter_copy(f, *first).wait_send()
            scatter_copy(f, *second).wait_send()
    for d in range(1, fronts):
        gather_copy(d).wait_send()
        gather2_copy(d).wait_send()
    for path in range(3):
        for d in range(fronts):
            spread_copy(path, d).wait_send()
    for k in range(levels):
        hyper_copy(k).wait_send()


def solution(mesh):
    leaves, fronts = mesh.shape["leaf"], mesh.shape["front"]
    levels = leaves.bit_length() - 1

    def on_device(child_left_factors, child_v, ranks, sketch, dinv, rhs):
        _, length, rank = child_left_factors.shape
        tiles = dinv.shape[1]
        sides = rhs.shape[1]
        used = rank + sides
        shard = 4 * rank // fronts
        shard2 = -(-used // (8 * fronts)) * 8
        vmem = pl.BlockSpec(memory_space=pltpu.VMEM)
        dma = pltpu.SemaphoreType.DMA
        return pl.pallas_call(
            functools.partial(kernel, leaves, fronts),
            out_shape=jax.ShapeDtypeStruct((1, sides, length), F32),
            in_specs=[pl.BlockSpec(memory_space=pltpu.SMEM)] + [vmem] * 5,
            out_specs=vmem,
            scratch_shapes=[
                pltpu.VMEM((4, length, rank), BF16),
                pltpu.VMEM((4, length, rank), BF16),
                pltpu.VMEM((4 * rank, rank), F32),
                pltpu.VMEM((fronts, shard, rank), F32),
                pltpu.VMEM((4, 4 * rank, rank), F32),
                pltpu.VMEM((2, rank, 2 * rank), F32),
                pltpu.VMEM((2, rank, rank), F32),
                pltpu.VMEM((2 * rank, 2 * rank), F32),
                pltpu.VMEM((shard2 * fronts, rank), F32),
                pltpu.VMEM((fronts, shard2, rank), F32),
                pltpu.VMEM((shard2 * fronts, rank), F32),
                pltpu.VMEM((levels, 2, used, rank), F32),
                pltpu.VMEM((sides, length), F32),
                dma((2, 3, tiles)),
                dma((2, 3, tiles)),
                dma((fronts,)),
                dma((fronts,)),
                dma((fronts,)),
                dma((fronts,)),
                dma((3, fronts)),
                dma((3, fronts)),
                dma((fronts,)),
                dma((fronts,)),
                dma((fronts,)),
                dma((fronts,)),
                dma((levels,)),
                dma((levels,)),
            ],
            compiler_params=pltpu.CompilerParams(
                collective_id=0, has_side_effects=True, vmem_limit_bytes=40 * 1024 * 1024
            ),
        )(ranks, child_left_factors, child_v, sketch, dinv, rhs)

    placed = (
        P("leaf", "front", None),
        P("leaf", "front", None),
        P("leaf", "front"),
        P("front", None),
        P("leaf", "front", None, None),
        P("leaf", None, "front"),
    )
    return jax.shard_map(
        on_device, mesh=mesh, in_specs=placed, out_specs=P("leaf", None, "front"), check_vma=False
    )
```

```python
import functools

import jax
import jax.numpy as jnp
from jax import lax
from jax.experimental import pallas as pl
from jax.experimental.pallas import tpu as pltpu
from jax.sharding import PartitionSpec as P

MESH = pl.DeviceIdType.MESH
F32 = jnp.float32
BF16 = jnp.bfloat16
PANEL = 16


def dot(a, b):
    return jnp.dot(a, b, preferred_element_type=F32)


def dot_nt(a, b):
    return lax.dot_general(a, b, (((1,), (1,)), ((), ())), preferred_element_type=F32)


def dot_tn(a, b):
    return lax.dot_general(a, b, (((0,), (0,)), ((), ())), preferred_element_type=F32)


def thirds(x):
    high = x.astype(BF16)
    rest = x - high.astype(F32)
    middle = rest.astype(BF16)
    return high, middle, (rest - middle.astype(F32)).astype(BF16)


def full(a, b, ca=1, cb=0):
    if a.dtype == BF16 and b.dtype == BF16:
        pa, pb = [a], [b]
    elif a.dtype == BF16:
        pa, pb = [a] * 3, thirds(b)
    elif b.dtype == BF16:
        pa, pb = thirds(a), [b] * 3
    else:
        (a1, a2, a3), (b1, b2, b3) = thirds(a), thirds(b)
        pa, pb = (a1, a2, a1, a3, a2, a1), (b1, b1, b2, b1, b2, b3)
    return lax.dot_general(
        jnp.concatenate(pa, axis=ca),
        jnp.concatenate(pb, axis=cb),
        (((ca,), (cb,)), ((), ())),
        preferred_element_type=F32,
    )


def halves(x):
    high = x.astype(BF16)
    return high, (x - high.astype(F32)).astype(BF16)


def flip(index, bit):
    return index + bit - 2 * bit * lax.rem(index // bit, 2)


def inverse_factors(grams, work, inverse):
    size = grams[0].shape[0]
    eye = (
        lax.broadcasted_iota(jnp.int32, (size, size), 0)
        == lax.broadcasted_iota(jnp.int32, (size, size), 1)
    ).astype(F32)
    for q, gram in enumerate(grams):
        work[q, :, :size] = gram
        work[q, :, size:] = eye
    lane = lax.broadcasted_iota(jnp.int32, (PANEL, size), 1)
    row = lax.broadcasted_iota(jnp.int32, (PANEL, size), 0)

    def step(b, carry):
        base = pl.multiple_of(b * PANEL, PANEL)
        for q in range(len(grams)):
            left = work[q, pl.ds(base, PANEL), :size]
            right = work[q, pl.ds(base, PANEL), size:]
            columns = [
                jnp.broadcast_to(
                    jnp.sum(jnp.where(lane == base + j, left, 0.0), axis=1, keepdims=True),
                    (PANEL, size),
                )
                for j in range(PANEL)
            ]
            pivots = jnp.zeros((PANEL, size), F32)
            for j in range(PANEL):
                pivots = jnp.where(row == j, columns[j], pivots)
                times = jnp.where(row > j, columns[j] * (1.0 / columns[j][j : j + 1, :]), 0.0)
                left = left - times * left[j : j + 1, :]
                right = right - times * right[j : j + 1, :]
                for k in range(j + 1, PANEL):
                    columns[k] = columns[k] - times * columns[k][j : j + 1, :]
            scale = lax.rsqrt(pivots)
            scale = scale * (1.5 - 0.5 * pivots * scale * scale)
            left = left * scale
            right = right * scale
            inverse[q, pl.ds(base, PANEL), :] = right
            below = jnp.where(lane >= base + PANEL, left, 0.0)
            work[q] -= full(below, jnp.concatenate([left, right], axis=1), 0, 0)
        return carry

    lax.fori_loop(0, size // PANEL, step, 0, unroll=True)


def kernel(
    leaves, fronts, rank_ref, u_ref, v_ref, sketch_ref, dinv_ref, rhs_ref, out_ref,
    uall, vall, strip, landed, gath, work, inverse, wide, part, landed2, whole, hyper, sol,
    a_send, a_recv, rs_send, rs_recv, ag_send, ag_recv, d_send, d_recv,
    rs2_send, rs2_recv, ag2_send, ag2_recv, h_send, h_recv,
):
    leaf = lax.axis_index("leaf")
    front = lax.axis_index("front")
    tiles, tile = dinv_ref.shape[1], dinv_ref.shape[2]
    rank = u_ref.shape[2]
    sides = rhs_ref.shape[1]
    levels = leaves.bit_length() - 1
    mine = lax.rem(leaf, 4)
    sibling, cousin = flip(leaf, 1), flip(leaf, 2)
    theirs, across = flip(mine, 1), flip(mine, 2)
    opposite = flip(theirs, 2)
    shard = strip.shape[0] // fronts
    shard2 = part.shape[0] // fronts

    barrier = pltpu.get_barrier_semaphore()
    for level in range(levels):
        pl.semaphore_signal(barrier, inc=1, device_id=(flip(leaf, 1 << level), front), device_id_type=MESH)
    for d in range(1, fronts):
        pl.semaphore_signal(barrier, inc=1, device_id=(leaf, lax.rem(front + d, fronts)), device_id_type=MESH)

    def rows(t):
        return pl.ds(t * tile, tile)

    column = lax.broadcasted_iota(jnp.int32, (tile, rank), 1)
    for t in range(tiles):
        keep = column < rank_ref[0, t]
        uall[mine, rows(t), :] = jnp.where(keep, u_ref[0, rows(t), :].astype(F32), 0.0).astype(BF16)
        vall[mine, rows(t), :] = v_ref[0, rows(t), :]
    pl.semaphore_wait(barrier, levels + fronts - 1)

    def remote(src, dst, send, recv, target):
        return pltpu.make_async_remote_copy(
            src_ref=src, dst_ref=dst, send_sem=send, recv_sem=recv, device_id=target, device_id_type=MESH
        )

    def factor_copy(kind, path, t):
        held = (uall, vall)[kind]
        block = held.at[across if path == 2 else mine, rows(t), :]
        target = (cousin if path == 1 else sibling, front)
        return remote(block, block, a_send.at[kind, path, t], a_recv.at[kind, path, t], target)

    for kind in range(2):
        for path in (1, 0):
            for t in range(tiles):
                factor_copy(kind, path, t).start()

    def scatter_copy(f, buffer, landing, size, send, recv):
        return remote(buffer.at[pl.ds(f * size, size), :], landing.at[front], send.at[f], recv.at[front], (leaf, f))

    def landing_wait(s, buffer, landing, size, send, recv):
        remote(buffer.at[pl.ds(0, size), :], landing.at[s], send.at[s], recv.at[s], (leaf, s)).wait_recv()

    first = (strip, landed, shard, rs_send, rs_recv)
    second = (part, landed2, shard2, rs2_send, rs2_recv)

    def scatter(lower, upper, what):
        for f in range(lower, upper):
            @pl.when(front != f)
            def _(f=f):
                scatter_copy(f, *what).start()

    own_t = uall[mine].T
    strip[pl.ds(0, rank), :] = dot_tn(vall[mine], sketch_ref[...])
    scatter(0, fronts // 4, first)
    strip[pl.ds(rank, rank), :] = dot(own_t, uall[mine])
    scatter(fronts // 4, fronts // 2, first)

    for t in range(tiles):
        sol[:, rows(t)] = dot_nt(rhs_ref[0, :, rows(t)], dinv_ref[0, t])

    for t in range(tiles):
        factor_copy(0, 1, t).wait_recv()
        factor_copy(0, 2, t).start()
    for t in range(tiles):
        factor_copy(0, 0, t).wait_recv()
    for t in range(tiles):
        factor_copy(0, 2, t).wait_recv()
    for j in (1, 2):
        strip[pl.ds((j + 1) * rank, rank), :] = dot(own_t, uall[lax.rem(mine + j, 4)])
        scatter((j + 1) * fronts // 4, (j + 2) * fronts // 4, first)

    def reduced(buffer, landing, size, send, recv):
        total = buffer[pl.ds(pl.multiple_of(front * size, 8), size), :]
        for s in range(fronts):
            @pl.when(front != s)
            def _(s=s):
                landing_wait(s, buffer, landing, size, send, recv)

            total = total + jnp.where(front != s, landing[s], 0.0)
        return total

    for s in range(fronts):
        @pl.when(front == s)
        def _(s=s):
            landed[s] = jnp.zeros(landed.shape[1:], F32)
            landed2[s] = jnp.zeros(landed2.shape[1:], F32)

    def piece(i, s):
        return gath.at[i, pl.ds(s * shard, shard), :]

    def gather_copy(d):
        return remote(
            piece(mine, front), piece(mine, front), ag_send.at[d], ag_recv.at[d], (leaf, lax.rem(front + d, fronts))
        )

    def spread_copy(path, d):
        block = piece(across if path == 2 else mine, lax.rem(front - d + fronts, fronts))
        target = (cousin if path == 1 else sibling, front)
        return remote(block, block, d_send.at[path, d], d_recv.at[path, d], target)

    gath[mine, pl.ds(pl.multiple_of(front * shard, 8), shard), :] = reduced(*first)
    for d in range(1, fronts):
        gather_copy(d).start()
    for d in range(fronts):
        if d:
            gather_copy(d).wait_recv()
        spread_copy(1, d).start()
        spread_copy(0, d).start()
    for t in range(tiles):
        factor_copy(1, 1, t).wait_recv()
        factor_copy(1, 2, t).start()
    for d in range(fronts):
        spread_copy(1, d).wait_recv()
        spread_copy(2, d).start()
    for d in range(fronts):
        spread_copy(0, d).wait_recv()
    for d in range(fronts):
        spread_copy(2, d).wait_recv()

    def block(i, j):
        return gath[i, pl.ds(j * rank, rank), :]

    def square(a, b, c, d):
        wide[pl.ds(0, rank), pl.ds(0, rank)] = a
        wide[pl.ds(0, rank), pl.ds(rank, rank)] = b
        wide[pl.ds(rank, rank), pl.ds(0, rank)] = c
        wide[pl.ds(rank, rank), pl.ds(rank, rank)] = d
        return wide[...]

    raw, small, cross, grams = [], [], [], []
    for p in range(2):
        a, b = 2 * p, 2 * p + 1
        between = block(a, 2)
        pair = square(block(a, 1), between, between.T, block(b, 1))
        raw.append(jnp.concatenate([block(a, 0), block(b, 0)], axis=0))
        small.append(raw[p].astype(BF16))
        cross.append(full(pair, small[p]))
        grams.append(full(small[p], cross[p], 0, 0))
    inverse_factors(grams, work, inverse)
    turn = [full(small[p], inverse[p], 1, 1) for p in range(2)]
    weight = [full(cross[p], inverse[p], 1, 1).astype(BF16) for p in range(2)]
    small2 = [full(weight[p], raw[p], 0, 0).astype(BF16) for p in range(2)]
    pair = square(block(0, 3), block(3, 2).T, block(1, 2), block(1, 3))
    middle = full(turn[0], full(pair, turn[1]), 0, 0)
    cross2 = [small2[0].astype(F32) + full(middle, small2[1]), full(middle, small2[0], 0, 0) + small2[1].astype(F32)]
    gram2 = full(small2[0], cross2[0], 0, 0) + full(small2[1], cross2[1], 0, 0)
    inverse_factors([gram2], work, inverse)
    turn2 = [halves(full(turn[p], full(small2[p], inverse[0], 1, 1))) for p in range(2)]
    weight2 = [
        halves(dot(weight[p], full(cross2[p], inverse[0], 1, 1).astype(BF16))) for p in range(2)
    ]

    def combined(held, factors):
        total = None
        for i in range(4):
            half = slice((i % 2) * rank, (i % 2 + 1) * rank)
            for part_of in factors[i // 2]:
                term = dot(held[i], part_of[half])
                total = term if total is None else total + term
        return total.astype(BF16)

    left_f = combined(uall, turn2)
    coupled = [dot(dinv_ref[0, t], left_f[t * tile : (t + 1) * tile]).astype(BF16) for t in range(tiles)]
    for path in (0, 2):
        for t in range(tiles):
            factor_copy(1, path, t).wait_recv()
    right_f = combined(vall, weight2)
    used = rank + sides
    if used < part.shape[0]:
        part[pl.ds(used, part.shape[0] - used), :] = jnp.zeros((part.shape[0] - used, rank), F32)
    part[pl.ds(0, rank), :] = -dot_tn(jnp.concatenate(coupled, axis=0), right_f)
    part[pl.ds(rank, sides), :] = dot(sol[...].astype(BF16), right_f)

    scatter(0, fronts, second)

    def piece2(s):
        return whole.at[pl.ds(s * shard2, shard2), :]

    def gather2_copy(d):
        return remote(
            piece2(front), piece2(front), ag2_send.at[d], ag2_recv.at[d], (leaf, lax.rem(front + d, fronts))
        )

    whole[pl.ds(pl.multiple_of(front * shard2, 16), shard2), :] = reduced(*second).astype(BF16)
    for d in range(1, fronts):
        gather2_copy(d).start()
    for d in range(1, fronts):
        gather2_copy(d).wait_recv()

    hyper[0, 0] = whole[pl.ds(0, used), :]
    low = lax.broadcasted_iota(jnp.int32, (used, rank), 0)
    along = lax.broadcasted_iota(jnp.int32, (used, rank), 1)
    prefix = jnp.where(low == along, 1.0, 0.0)

    def then(first_map, second_map):
        return full(first_map.astype(BF16), second_map[:rank]) + jnp.where(low >= rank, second_map.astype(F32), 0.0)

    def hyper_copy(k):
        send = pl.ds(0, used) if k < levels - 1 else pl.ds(rank, sides)
        return remote(
            hyper.at[k, 0, send, :], hyper.at[k, 1, send, :], h_send.at[k], h_recv.at[k], (flip(leaf, 1 << k), front)
        )

    previous = None
    for k in range(levels):
        hyper_copy(k).start()
        hyper_copy(k).wait_recv()
        upper = lax.rem(leaf // (1 << k), 2) == 1
        if k < levels - 1:
            here, there = hyper[k, 0].astype(F32), hyper[k, 1].astype(F32)
            hyper[k + 1, 0] = then(jnp.where(upper, there, here), jnp.where(upper, here, there).astype(BF16)).astype(BF16)
            prefix = jnp.where(upper, then(there, prefix), prefix)
        else:
            there = hyper[k, 1, pl.ds(rank, sides), :]
            previous = prefix[rank:] + jnp.where(upper, full(there, prefix[:rank]), 0.0)

    for t in range(tiles):
        total = sol[:, rows(t)]
        for part_of in halves(previous):
            total = total - dot_nt(part_of, coupled[t])
        out_ref[0, :, rows(t)] = total

    for kind in range(2):
        for path in range(3):
            for t in range(tiles):
                factor_copy(kind, path, t).wait_send()
    for f in range(fronts):
        @pl.when(front != f)
        def _(f=f):
            scatter_copy(f, *first).wait_send()
            scatter_copy(f, *second).wait_send()
    for d in range(1, fronts):
        gather_copy(d).wait_send()
        gather2_copy(d).wait_send()
    for path in range(3):
        for d in range(fronts):
            spread_copy(path, d).wait_send()
    for k in range(levels):
        hyper_copy(k).wait_send()


def solution(mesh):
    leaves, fronts = mesh.shape["leaf"], mesh.shape["front"]
    levels = leaves.bit_length() - 1

    def on_device(child_left_factors, child_v, ranks, sketch, dinv, rhs):
        _, length, rank = child_left_factors.shape
        tiles = dinv.shape[1]
        sides = rhs.shape[1]
        used = rank + sides
        shard = 4 * rank // fronts
        shard2 = -(-used // (16 * fronts)) * 16
        vmem = pl.BlockSpec(memory_space=pltpu.VMEM)
        dma = pltpu.SemaphoreType.DMA
        return pl.pallas_call(
            functools.partial(kernel, leaves, fronts),
            out_shape=jax.ShapeDtypeStruct((1, sides, length), F32),
            in_specs=[pl.BlockSpec(memory_space=pltpu.SMEM)] + [vmem] * 5,
            out_specs=vmem,
            scratch_shapes=[
                pltpu.VMEM((4, length, rank), BF16),
                pltpu.VMEM((4, length, rank), BF16),
                pltpu.VMEM((4 * rank, rank), F32),
                pltpu.VMEM((fronts, shard, rank), F32),
                pltpu.VMEM((4, 4 * rank, rank), F32),
                pltpu.VMEM((2, rank, 2 * rank), F32),
                pltpu.VMEM((2, rank, rank), F32),
                pltpu.VMEM((2 * rank, 2 * rank), F32),
                pltpu.VMEM((shard2 * fronts, rank), F32),
                pltpu.VMEM((fronts, shard2, rank), F32),
                pltpu.VMEM((shard2 * fronts, rank), BF16),
                pltpu.VMEM((levels, 2, used, rank), BF16),
                pltpu.VMEM((sides, length), F32),
                dma((2, 3, tiles)),
                dma((2, 3, tiles)),
                dma((fronts,)),
                dma((fronts,)),
                dma((fronts,)),
                dma((fronts,)),
                dma((3, fronts)),
                dma((3, fronts)),
                dma((fronts,)),
                dma((fronts,)),
                dma((fronts,)),
                dma((fronts,)),
                dma((levels,)),
                dma((levels,)),
            ],
            compiler_params=pltpu.CompilerParams(
                collective_id=0, has_side_effects=True, vmem_limit_bytes=40 * 1024 * 1024
            ),
        )(ranks, child_left_factors, child_v, sketch, dinv, rhs)

    placed = (
        P("leaf", "front", None),
        P("leaf", "front", None),
        P("leaf", "front"),
        P("front", None),
        P("leaf", "front", None, None),
        P("leaf", None, "front"),
    )
    return jax.shard_map(
        on_device, mesh=mesh, in_specs=placed, out_specs=P("leaf", None, "front"), check_vma=False
    )
```

```python
import functools

import jax
import jax.numpy as jnp
from jax import lax
from jax.experimental import pallas as pl
from jax.experimental.pallas import tpu as pltpu
from jax.sharding import PartitionSpec as P

MESH = pl.DeviceIdType.MESH
F32 = jnp.float32
BF16 = jnp.bfloat16
PANEL = 16


def dot(a, b):
    return jnp.dot(a, b, preferred_element_type=F32)


def dot_nt(a, b):
    return lax.dot_general(a, b, (((1,), (1,)), ((), ())), preferred_element_type=F32)


def dot_tn(a, b):
    return lax.dot_general(a, b, (((0,), (0,)), ((), ())), preferred_element_type=F32)


def thirds(x):
    high = x.astype(BF16)
    rest = x - high.astype(F32)
    middle = rest.astype(BF16)
    return high, middle, (rest - middle.astype(F32)).astype(BF16)


def full(a, b, ca=1, cb=0):
    if a.dtype == BF16 and b.dtype == BF16:
        pa, pb = [a], [b]
    elif a.dtype == BF16:
        pa, pb = [a] * 3, thirds(b)
    elif b.dtype == BF16:
        pa, pb = thirds(a), [b] * 3
    else:
        (a1, a2, a3), (b1, b2, b3) = thirds(a), thirds(b)
        pa, pb = (a1, a2, a1, a3, a2, a1), (b1, b1, b2, b1, b2, b3)
    return lax.dot_general(
        jnp.concatenate(pa, axis=ca),
        jnp.concatenate(pb, axis=cb),
        (((ca,), (cb,)), ((), ())),
        preferred_element_type=F32,
    )


def halves(x):
    high = x.astype(BF16)
    return high, (x - high.astype(F32)).astype(BF16)


def flip(index, bit):
    return index + bit - 2 * bit * lax.rem(index // bit, 2)


def inverse_factors(grams, work, inverse):
    size = grams[0].shape[0]
    eye = (
        lax.broadcasted_iota(jnp.int32, (size, size), 0)
        == lax.broadcasted_iota(jnp.int32, (size, size), 1)
    ).astype(F32)
    for q, gram in enumerate(grams):
        work[q, :, :size] = gram
        work[q, :, size:] = eye
    lane = lax.broadcasted_iota(jnp.int32, (PANEL, size), 1)
    row = lax.broadcasted_iota(jnp.int32, (PANEL, size), 0)

    def step(b, carry):
        base = pl.multiple_of(b * PANEL, PANEL)
        for q in range(len(grams)):
            left = work[q, pl.ds(base, PANEL), :size]
            right = work[q, pl.ds(base, PANEL), size:]
            columns = [
                jnp.broadcast_to(
                    jnp.sum(jnp.where(lane == base + j, left, 0.0), axis=1, keepdims=True),
                    (PANEL, size),
                )
                for j in range(PANEL)
            ]
            pivots = jnp.zeros((PANEL, size), F32)
            for j in range(PANEL):
                pivots = jnp.where(row == j, columns[j], pivots)
                times = jnp.where(row > j, columns[j] * (1.0 / columns[j][j : j + 1, :]), 0.0)
                left = left - times * left[j : j + 1, :]
                right = right - times * right[j : j + 1, :]
                for k in range(j + 1, PANEL):
                    columns[k] = columns[k] - times * columns[k][j : j + 1, :]
            scale = lax.rsqrt(pivots)
            scale = scale * (1.5 - 0.5 * pivots * scale * scale)
            left = left * scale
            right = right * scale
            inverse[q, pl.ds(base, PANEL), :] = right
            below = jnp.where(lane >= base + PANEL, left, 0.0)
            work[q] -= full(below, jnp.concatenate([left, right], axis=1), 0, 0)
        return carry

    lax.fori_loop(0, size // PANEL, step, 0, unroll=True)


def kernel(
    leaves, fronts, rank_ref, u_ref, v_ref, sketch_ref, dinv_ref, rhs_ref, out_ref,
    uall, vall, strip, landed, gath, work, inverse, wide, part, landed2, whole, hyper, sol,
    a_send, a_recv, rs_send, rs_recv, ag_send, ag_recv, d_send, d_recv,
    rs2_send, rs2_recv, ag2_send, ag2_recv, h_send, h_recv,
):
    leaf = lax.axis_index("leaf")
    front = lax.axis_index("front")
    tiles, tile = dinv_ref.shape[1], dinv_ref.shape[2]
    rank = u_ref.shape[2]
    sides = rhs_ref.shape[1]
    levels = leaves.bit_length() - 1
    mine = lax.rem(leaf, 4)
    sibling, cousin = flip(leaf, 1), flip(leaf, 2)
    theirs, across = flip(mine, 1), flip(mine, 2)
    opposite = flip(theirs, 2)
    shard = strip.shape[0] // fronts
    shard2 = part.shape[0] // fronts

    barrier = pltpu.get_barrier_semaphore()
    for level in range(levels):
        pl.semaphore_signal(barrier, inc=1, device_id=(flip(leaf, 1 << level), front), device_id_type=MESH)
    for d in range(1, fronts):
        pl.semaphore_signal(barrier, inc=1, device_id=(leaf, lax.rem(front + d, fronts)), device_id_type=MESH)

    def rows(t):
        return pl.ds(t * tile, tile)

    column = lax.broadcasted_iota(jnp.int32, (tile, rank), 1)
    for t in range(tiles):
        keep = column < rank_ref[0, t]
        uall[mine, rows(t), :] = jnp.where(keep, u_ref[0, rows(t), :].astype(F32), 0.0).astype(BF16)
        vall[mine, rows(t), :] = v_ref[0, rows(t), :]
    pl.semaphore_wait(barrier, levels + fronts - 1)

    def remote(src, dst, send, recv, target):
        return pltpu.make_async_remote_copy(
            src_ref=src, dst_ref=dst, send_sem=send, recv_sem=recv, device_id=target, device_id_type=MESH
        )

    def factor_copy(kind, path, t):
        held = (uall, vall)[kind]
        block = held.at[across if path == 2 else mine, rows(t), :]
        target = (cousin if path == 1 else sibling, front)
        return remote(block, block, a_send.at[kind, path, t], a_recv.at[kind, path, t], target)

    for kind in range(2):
        for path in (1, 0):
            for t in range(tiles):
                factor_copy(kind, path, t).start()

    def scatter_copy(f, buffer, landing, size, send, recv):
        return remote(buffer.at[pl.ds(f * size, size), :], landing.at[front], send.at[f], recv.at[front], (leaf, f))

    def landing_wait(s, buffer, landing, size, send, recv):
        remote(buffer.at[pl.ds(0, size), :], landing.at[s], send.at[s], recv.at[s], (leaf, s)).wait_recv()

    first = (strip, landed, shard, rs_send, rs_recv)
    second = (part, landed2, shard2, rs2_send, rs2_recv)

    def scatter(lower, upper, what):
        for f in range(lower, upper):
            @pl.when(front != f)
            def _(f=f):
                scatter_copy(f, *what).start()

    own_t = uall[mine].T
    strip[pl.ds(0, rank), :] = dot_tn(vall[mine], sketch_ref[...])
    scatter(0, fronts // 4, first)
    strip[pl.ds(rank, rank), :] = dot(own_t, uall[mine])
    scatter(fronts // 4, fronts // 2, first)

    for t in range(tiles):
        sol[:, rows(t)] = dot_nt(rhs_ref[0, :, rows(t)], dinv_ref[0, t])

    for t in range(tiles):
        factor_copy(0, 1, t).wait_recv()
        factor_copy(0, 2, t).start()
    for t in range(tiles):
        factor_copy(0, 0, t).wait_recv()
    for t in range(tiles):
        factor_copy(0, 2, t).wait_recv()
    for j in (1, 2):
        strip[pl.ds((j + 1) * rank, rank), :] = dot(own_t, uall[lax.rem(mine + j, 4)])
        scatter((j + 1) * fronts // 4, (j + 2) * fronts // 4, first)

    def reduced(buffer, landing, size, send, recv):
        total = buffer[pl.ds(pl.multiple_of(front * size, 16), size), :].astype(F32)
        for s in range(fronts):
            @pl.when(front != s)
            def _(s=s):
                landing_wait(s, buffer, landing, size, send, recv)

            total = total + jnp.where(front != s, landing[s].astype(F32), 0.0)
        return total

    for s in range(fronts):
        @pl.when(front == s)
        def _(s=s):
            landed[s] = jnp.zeros(landed.shape[1:], F32)
            landed2[s] = jnp.zeros(landed2.shape[1:], BF16)

    def piece(i, s):
        return gath.at[i, pl.ds(s * shard, shard), :]

    def gather_copy(d):
        return remote(
            piece(mine, front), piece(mine, front), ag_send.at[d], ag_recv.at[d], (leaf, lax.rem(front + d, fronts))
        )

    def spread_copy(path, d):
        block = piece(across if path == 2 else mine, lax.rem(front - d + fronts, fronts))
        target = (cousin if path == 1 else sibling, front)
        return remote(block, block, d_send.at[path, d], d_recv.at[path, d], target)

    gath[mine, pl.ds(pl.multiple_of(front * shard, 8), shard), :] = reduced(*first)
    for d in range(1, fronts):
        gather_copy(d).start()
    for d in range(fronts):
        if d:
            gather_copy(d).wait_recv()
        spread_copy(1, d).start()
        spread_copy(0, d).start()
    for t in range(tiles):
        factor_copy(1, 1, t).wait_recv()
        factor_copy(1, 2, t).start()
    for d in range(fronts):
        spread_copy(1, d).wait_recv()
        spread_copy(2, d).start()
    for d in range(fronts):
        spread_copy(0, d).wait_recv()
    for d in range(fronts):
        spread_copy(2, d).wait_recv()

    def block(i, j):
        return gath[i, pl.ds(j * rank, rank), :]

    def square(a, b, c, d):
        wide[pl.ds(0, rank), pl.ds(0, rank)] = a
        wide[pl.ds(0, rank), pl.ds(rank, rank)] = b
        wide[pl.ds(rank, rank), pl.ds(0, rank)] = c
        wide[pl.ds(rank, rank), pl.ds(rank, rank)] = d
        return wide[...]

    raw, small, cross, grams = [], [], [], []
    for p in range(2):
        a, b = 2 * p, 2 * p + 1
        between = block(a, 2)
        pair = square(block(a, 1), between, between.T, block(b, 1))
        raw.append(jnp.concatenate([block(a, 0), block(b, 0)], axis=0))
        small.append(raw[p].astype(BF16))
        cross.append(full(pair, small[p]))
        grams.append(full(small[p], cross[p], 0, 0))
    inverse_factors(grams, work, inverse)
    turn = [full(small[p], inverse[p], 1, 1) for p in range(2)]
    weight = [full(cross[p], inverse[p], 1, 1).astype(BF16) for p in range(2)]
    small2 = [full(weight[p], raw[p], 0, 0).astype(BF16) for p in range(2)]
    pair = square(block(0, 3), block(3, 2).T, block(1, 2), block(1, 3))
    middle = full(turn[0], full(pair, turn[1]), 0, 0)
    cross2 = [small2[0].astype(F32) + full(middle, small2[1]), full(middle, small2[0], 0, 0) + small2[1].astype(F32)]
    gram2 = full(small2[0], cross2[0], 0, 0) + full(small2[1], cross2[1], 0, 0)
    inverse_factors([gram2], work, inverse)
    turn2 = [halves(full(turn[p], full(small2[p], inverse[0], 1, 1))) for p in range(2)]
    weight2 = [
        halves(dot(weight[p], full(cross2[p], inverse[0], 1, 1).astype(BF16))) for p in range(2)
    ]

    def combined(held, factors):
        total = None
        for i in range(4):
            half = slice((i % 2) * rank, (i % 2 + 1) * rank)
            for part_of in factors[i // 2]:
                term = dot(held[i], part_of[half])
                total = term if total is None else total + term
        return total.astype(BF16)

    left_f = combined(uall, turn2)
    coupled = [dot(dinv_ref[0, t], left_f[t * tile : (t + 1) * tile]).astype(BF16) for t in range(tiles)]
    for path in (0, 2):
        for t in range(tiles):
            factor_copy(1, path, t).wait_recv()
    right_f = combined(vall, weight2)
    used = rank + sides
    if used < part.shape[0]:
        part[pl.ds(used, part.shape[0] - used), :] = jnp.zeros((part.shape[0] - used, rank), BF16)
    part[pl.ds(0, rank), :] = (-dot_tn(jnp.concatenate(coupled, axis=0), right_f)).astype(BF16)
    part[pl.ds(rank, sides), :] = dot(sol[...].astype(BF16), right_f).astype(BF16)

    scatter(0, fronts, second)

    def piece2(s):
        return whole.at[pl.ds(s * shard2, shard2), :]

    def gather2_copy(d):
        return remote(
            piece2(front), piece2(front), ag2_send.at[d], ag2_recv.at[d], (leaf, lax.rem(front + d, fronts))
        )

    whole[pl.ds(pl.multiple_of(front * shard2, 16), shard2), :] = reduced(*second).astype(BF16)
    for d in range(1, fronts):
        gather2_copy(d).start()
    for d in range(1, fronts):
        gather2_copy(d).wait_recv()

    hyper[0, 0] = whole[pl.ds(0, used), :]
    low = lax.broadcasted_iota(jnp.int32, (used, rank), 0)
    along = lax.broadcasted_iota(jnp.int32, (used, rank), 1)
    prefix = jnp.where(low == along, 1.0, 0.0)

    def then(first_map, second_map):
        return full(first_map.astype(BF16), second_map[:rank]) + jnp.where(low >= rank, second_map.astype(F32), 0.0)

    def hyper_copy(k):
        send = pl.ds(0, used) if k < levels - 1 else pl.ds(rank, sides)
        return remote(
            hyper.at[k, 0, send, :], hyper.at[k, 1, send, :], h_send.at[k], h_recv.at[k], (flip(leaf, 1 << k), front)
        )

    previous = None
    for k in range(levels):
        hyper_copy(k).start()
        hyper_copy(k).wait_recv()
        upper = lax.rem(leaf // (1 << k), 2) == 1
        if k < levels - 1:
            here, there = hyper[k, 0].astype(F32), hyper[k, 1].astype(F32)
            hyper[k + 1, 0] = then(jnp.where(upper, there, here), jnp.where(upper, here, there).astype(BF16)).astype(BF16)
            prefix = jnp.where(upper, then(there, prefix), prefix)
        else:
            there = hyper[k, 1, pl.ds(rank, sides), :]
            previous = prefix[rank:] + jnp.where(upper, full(there, prefix[:rank]), 0.0)

    for t in range(tiles):
        total = sol[:, rows(t)]
        for part_of in halves(previous):
            total = total - dot_nt(part_of, coupled[t])
        out_ref[0, :, rows(t)] = total

    for kind in range(2):
        for path in range(3):
            for t in range(tiles):
                factor_copy(kind, path, t).wait_send()
    for f in range(fronts):
        @pl.when(front != f)
        def _(f=f):
            scatter_copy(f, *first).wait_send()
            scatter_copy(f, *second).wait_send()
    for d in range(1, fronts):
        gather_copy(d).wait_send()
        gather2_copy(d).wait_send()
    for path in range(3):
        for d in range(fronts):
            spread_copy(path, d).wait_send()
    for k in range(levels):
        hyper_copy(k).wait_send()


def solution(mesh):
    leaves, fronts = mesh.shape["leaf"], mesh.shape["front"]
    levels = leaves.bit_length() - 1

    def on_device(child_left_factors, child_v, ranks, sketch, dinv, rhs):
        _, length, rank = child_left_factors.shape
        tiles = dinv.shape[1]
        sides = rhs.shape[1]
        used = rank + sides
        shard = 4 * rank // fronts
        shard2 = -(-used // (16 * fronts)) * 16
        vmem = pl.BlockSpec(memory_space=pltpu.VMEM)
        dma = pltpu.SemaphoreType.DMA
        return pl.pallas_call(
            functools.partial(kernel, leaves, fronts),
            out_shape=jax.ShapeDtypeStruct((1, sides, length), F32),
            in_specs=[pl.BlockSpec(memory_space=pltpu.SMEM)] + [vmem] * 5,
            out_specs=vmem,
            scratch_shapes=[
                pltpu.VMEM((4, length, rank), BF16),
                pltpu.VMEM((4, length, rank), BF16),
                pltpu.VMEM((4 * rank, rank), F32),
                pltpu.VMEM((fronts, shard, rank), F32),
                pltpu.VMEM((4, 4 * rank, rank), F32),
                pltpu.VMEM((2, rank, 2 * rank), F32),
                pltpu.VMEM((2, rank, rank), F32),
                pltpu.VMEM((2 * rank, 2 * rank), F32),
                pltpu.VMEM((shard2 * fronts, rank), BF16),
                pltpu.VMEM((fronts, shard2, rank), BF16),
                pltpu.VMEM((shard2 * fronts, rank), BF16),
                pltpu.VMEM((levels, 2, used, rank), BF16),
                pltpu.VMEM((sides, length), F32),
                dma((2, 3, tiles)),
                dma((2, 3, tiles)),
                dma((fronts,)),
                dma((fronts,)),
                dma((fronts,)),
                dma((fronts,)),
                dma((3, fronts)),
                dma((3, fronts)),
                dma((fronts,)),
                dma((fronts,)),
                dma((fronts,)),
                dma((fronts,)),
                dma((levels,)),
                dma((levels,)),
            ],
            compiler_params=pltpu.CompilerParams(
                collective_id=0, has_side_effects=True, vmem_limit_bytes=40 * 1024 * 1024
            ),
        )(ranks, child_left_factors, child_v, sketch, dinv, rhs)

    placed = (
        P("leaf", "front", None),
        P("leaf", "front", None),
        P("leaf", "front"),
        P("front", None),
        P("leaf", "front", None, None),
        P("leaf", None, "front"),
    )
    return jax.shard_map(
        on_device, mesh=mesh, in_specs=placed, out_specs=P("leaf", None, "front"), check_vma=False
    )
```
